32 devices in a mesh: row: 8 (over z, y), col: 4 (over x, core).
Axes of the slice: x: 2, y: 2, z: 4, core: 2. Of those that a mesh axis runs over, the one named last changes fastest.
Arguments:
- noise: float32 [2, 3072, 512], P(None, 'row', 'col'), may hold values from -6 to 6
- kappa: float32 [3072, 512], P('row', 'col'), may hold values from 0.2 to 1
- metric: float32 [3072, 512], P('row', 'col'), may hold values from 0.3 to 1
- edge_src: int32 [24], replicated, may hold values from 0 to 23, each once
- edge_rev: int32 [24], replicated, may hold values from 0 to 1
- corner_src: int32 [24], replicated, may hold values from 0 to 47
Outputs:
- sample: float32 [2, 3072, 512], P(None, 'row', 'col')
The draws below stay inside these ranges and needn't reach their ends.
Inputs may be any that keep to these rules, and one draw needn't show every extreme that they name: `edge_src`: every line number appears once.
All inputs are finite; a program needn't handle non-finite values.
Results may differ from the reference program's by a relative error of at most 0.00011.
Values sent between devices are 32-bit elements; how exact they have to be, the bound alone decides.
A program may use at most 64 MiB of HBM per device.

```python
import math
import jax
import jax.numpy as jnp

LEVELS = 2
SWEEPS = 4
FACE = 512


def with_ends(values, key, low, high):
    longest = values.shape.index(max(values.shape))
    spots = []
    for shift in (0, 1):
        where = [jax.random.randint(jax.random.fold_in(key, axis), (), 0, length) for axis, length in enumerate(values.shape)]
        where[longest] = (where[longest] + shift) % values.shape[longest]
        spots.append(tuple(where))
    return values.at[spots[0]].set(low).at[spots[1]].set(high)


def levels(key, dims, split, smallest, high):
    factor_of = 1.0
    for dim, parts in split:
        heights = jax.random.uniform(jax.random.fold_in(jax.random.fold_in(key, 6), dim), (parts,), jnp.float32, smallest / len(split), high / len(split))
        factor_of = factor_of * jnp.repeat(jnp.exp(heights), dims[dim] // parts).reshape((-1,) + (1,) * (len(dims) - 1 - dim))
    return factor_of


def normal_values(key, shape, scale, most, pieces=(), kind=jnp.bfloat16):
    factor_of = levels(key, shape, pieces, -0.22, 0.18) if pieces else 1.0
    array = jax.random.normal(key, shape, jnp.float32) * scale * factor_of
    return jnp.minimum(jnp.maximum(array, -most), most).astype(kind)


def setup_inputs(seed: int = 0) -> dict:
    key_list = jax.random.split(jax.random.key(seed), 7)
    return {
        "noise": normal_values(key_list[0], (LEVELS, 6 * FACE, FACE), 1.0, 6.0, ((1, 8), (2, 4)), jnp.float32),
        "kappa": jnp.clip(jnp.exp(math.log(1.0) - 1.609438 * jax.random.uniform(key_list[1], (6 * FACE, FACE), jnp.float32) ** levels(key_list[1], (6 * FACE, FACE), ((0, 8), (1, 4)), -0.2, 0.2)), 0.2, 1.0),
        "metric": jnp.clip(jnp.exp(math.log(1.0) - 1.2039728 * jax.random.uniform(key_list[2], (6 * FACE, FACE), jnp.float32) ** levels(key_list[2], (6 * FACE, FACE), ((0, 8), (1, 4)), -0.2, 0.2)), 0.3, 1.0),
        "edge_src": jax.random.permutation(key_list[3], 24).astype(jnp.int32),
        "edge_rev": with_ends(jax.random.randint(key_list[4], (24,), 0, 2), jax.random.fold_in(key_list[4], 1), 0, 1).astype(jnp.int32),
        "corner_src": with_ends(jax.random.randint(key_list[5], (24,), 0, 48), jax.random.fold_in(key_list[5], 1), 0, 47).astype(jnp.int32),
    }


def reference(noise, kappa, metric, edge_src, edge_rev, corner_src):
    offset = FACE // 2
    rate_map = jnp.roll(kappa * metric * 0.125, offset, axis=0).reshape(6, FACE, FACE)
    field_now = jnp.roll(noise, offset, axis=1).reshape(LEVELS, 6, FACE, FACE)
    for sweep in range(SWEEPS):
        borders = jnp.stack([field_now[:, :, 0, :], field_now[:, :, FACE - 1, :], field_now[:, :, :, 0], field_now[:, :, :, FACE - 1]], axis=2)
        line_set = borders.transpose(1, 2, 0, 3).reshape(24, LEVELS, FACE)
        ghosts = line_set[edge_src]
        ghosts = jnp.where(edge_rev[:, None, None] == 1, ghosts[:, :, ::-1], ghosts).reshape(6, 4, LEVELS, FACE)
        line_ends = jnp.stack([line_set[:, :, 0], line_set[:, :, FACE - 1]], axis=1).reshape(48, LEVELS)
        corners = line_ends[corner_src].reshape(6, 4, LEVELS).transpose(1, 2, 0)
        padded = jnp.zeros((LEVELS, 6, FACE + 2, FACE + 2), jnp.float32)
        padded = padded.at[:, :, 1:-1, 1:-1].set(field_now)
        padded = padded.at[:, :, 0, 1:-1].set(ghosts[:, 0].transpose(1, 0, 2))
        padded = padded.at[:, :, FACE + 1, 1:-1].set(ghosts[:, 1].transpose(1, 0, 2))
        padded = padded.at[:, :, 1:-1, 0].set(ghosts[:, 2].transpose(1, 0, 2))
        padded = padded.at[:, :, 1:-1, FACE + 1].set(ghosts[:, 3].transpose(1, 0, 2))
        padded = padded.at[:, :, 0, 0].set(corners[0])
        padded = padded.at[:, :, 0, FACE + 1].set(corners[1])
        padded = padded.at[:, :, FACE + 1, 0].set(corners[2])
        padded = padded.at[:, :, FACE + 1, FACE + 1].set(corners[3])
        neighbours = padded[:, :, 0:-2, 0:-2] + padded[:, :, 0:-2, 1:-1] + padded[:, :, 0:-2, 2:]
        neighbours = neighbours + padded[:, :, 1:-1, 0:-2] + padded[:, :, 1:-1, 2:]
        neighbours = neighbours + padded[:, :, 2:, 0:-2] + padded[:, :, 2:, 1:-1] + padded[:, :, 2:, 2:]
        field_now = field_now + rate_map * (neighbours - 8.0 * field_now)
    return jnp.roll(field_now.reshape(LEVELS, 6 * FACE, FACE), -offset, axis=1)
```

```python
import functools
import math

import jax
import jax.numpy as jnp
from jax import lax
from jax.experimental import pallas as pl
from jax.experimental.pallas import tpu as pltpu
from jax.sharding import PartitionSpec as P

SWEEPS = 4
LANES = 128
MESH = pl.DeviceIdType.MESH


def kernel(
    dims, noise, kappa, metric, esrc, erev, csrc, out,
    field, rate, area, hsum, picked, flags, cols, *rest
):
    levels, rows, width, nr, nc = dims
    packs, stages, halos = rest[0:4], rest[4:8], rest[8:12]
    in_sem, pack_send, pack_recv, halo_send, halo_recv = rest[12:17]
    ndev = nr * nc
    face = width * nc
    total = 6 * face
    offset = face // 2
    unit = math.gcd(math.gcd(rows, offset), width)
    nu = rows // unit
    nw = width // unit
    per_face = face // unit
    short, full = 2 * nw, 2 * nw + nu

    i = lax.axis_index("row")
    c = lax.axis_index("col")
    me = i * nc + c
    left = c == 0
    right = c == nc - 1
    side = jnp.logical_or(left, right)

    loads = [
        pltpu.make_async_copy(noise, field, in_sem.at[0]),
        pltpu.make_async_copy(kappa, rate, in_sem.at[1]),
        pltpu.make_async_copy(metric, area, in_sem.at[2]),
    ]
    for load in loads:
        load.start()

    barrier = pltpu.get_barrier_semaphore()

    def greet(k, carry):
        d = lax.rem(me + k, ndev)
        pl.semaphore_signal(
            barrier, inc=1, device_id=(lax.div(d, nc), lax.rem(d, nc)), device_id_type=MESH
        )
        return carry

    lax.fori_loop(1, ndev, greet, 0)

    start = lax.rem(i * rows + offset, total)
    f0 = lax.div(start, face)
    into = start - f0 * face
    has_top = jnp.logical_or(into == 0, into + rows > face)
    has_bottom = into + rows >= face
    top_face = jnp.where(into == 0, f0, lax.rem(f0 + 1, 6))
    top_row = jnp.where(into == 0, 0, face - into)
    bottom_row = face - 1 - into
    top_at = jnp.where(has_top, top_row, 0)
    bottom_at = jnp.where(has_bottom, bottom_row, 0)
    top_hit = jnp.where(has_top, top_row, -1)
    bottom_hit = jnp.where(has_bottom, bottom_row, -1)

    def place(line, u):
        f = lax.div(line, 4)
        e = lax.rem(line, 4)
        row_stored = lax.rem(f * face + jnp.where(e == 1, face - 1, 0) + total - offset, total)
        row_at = (lax.div(row_stored, rows) * nc + lax.div(u, nw)) * full + e * nw + lax.rem(u, nw)
        side_stored = lax.rem(f * face + u * unit + total - offset, total)
        d = lax.div(side_stored, rows)
        k = lax.div(side_stored - d * rows, unit)
        side_at = (d * nc + jnp.where(e == 3, nc - 1, 0)) * full + short + k
        return jnp.where(e < 2, row_at, side_at)

    def ghost_unit(edge, u):
        turned = erev[edge]
        return place(esrc[edge], jnp.where(turned == 1, per_face - 1 - u, u)), turned

    def corner(index):
        s = csrc[index]
        end = lax.rem(s, 2)
        return place(lax.div(s, 2), end * (per_face - 1)), end

    def ghost_cell(edge, u, end):
        turned = erev[edge]
        at = place(esrc[edge], jnp.where(turned == 1, per_face - 1 - u, u))
        return at, jnp.where(turned == 1, 1 - end, end)

    def choose(flag, a, b):
        return jnp.where(flag, a[0], b[0]), jnp.where(flag, a[1], b[1])

    items = []
    bottom_face = f0
    for f, e, q0 in ((top_face, 0, 0), (bottom_face, 1, 2)):
        edge = 4 * f + e
        for k in range(nw):
            items.append(ghost_unit(edge, c * nw + k))
        before = ghost_cell(edge, jnp.maximum(c * nw - 1, 0), 1)
        after = ghost_cell(edge, jnp.minimum(c * nw + nw, per_face - 1), 0)
        items.append(choose(left, corner(4 * f + q0), before))
        items.append(choose(right, corner(4 * f + q0 + 1), after))
    side_edge = jnp.where(left, 2, 3)
    for k in range(nu):
        at = lax.rem(start + k * unit, total)
        f = lax.div(at, face)
        items.append(ghost_unit(4 * f + side_edge, lax.div(at - f * face, unit)))
    at = lax.rem(start + total - unit, total)
    f = lax.div(at, face)
    items.append(ghost_cell(4 * f + side_edge, lax.div(at - f * face, unit), 1))
    at = lax.rem(start + rows, total)
    f = lax.div(at, face)
    items.append(ghost_cell(4 * f + side_edge, lax.div(at - f * face, unit), 0))
    top0, bottom0, side0 = 0, nw + 2, 2 * (nw + 2)
    up_cell, down_cell = side0 + nu, side0 + nu + 1
    for n, (_, flip) in enumerate(items):
        flags[n * levels : (n + 1) * levels, :] = jnp.full((levels, LANES), flip, jnp.int32)

    lane = lax.broadcasted_iota(jnp.int32, (unit, LANES), 1)
    local_row = lax.broadcasted_iota(jnp.int32, (unit, LANES), 0)
    small_lane = lax.broadcasted_iota(jnp.int32, (8, LANES), 1)
    turn = lax.rem(
        unit - 1 - lax.broadcasted_iota(jnp.int32, (picked.shape[0], LANES), 1) + LANES, LANES
    )

    base = me * full
    up = lax.rem(i + nr - 1, nr)
    down = lax.rem(i + 1, nr)
    west = lax.rem(c + nc - 1, nc)
    east = lax.rem(c + 1, nc)

    def prepare(s):
        pack, stage = packs[s], stages[s]
        for l in range(levels):
            stage[0, l : l + 1, :] = field[l, 0:1, :]
            stage[1, l : l + 1, :] = field[l, rows - 1 : rows, :]
            for e, row in ((0, top_at), (1, bottom_at)):
                line = field[l, pl.ds(row, 1), :]
                for k in range(nw):
                    part = line if k == 0 else jnp.roll(line, -k * unit, axis=1)
                    pack[base + e * nw + k, l : l + 1, :] = part
        for k in range(nu):
            both = jnp.zeros((unit, LANES), jnp.float32)
            for l in range(levels):
                block = field[l, k * unit : (k + 1) * unit, :]
                both = jnp.where(lane >= 2 * l, pltpu.roll(block, 1 + 2 * l, 1), both)
            turned = both.T
            for l in range(levels):
                last = turned[2 * l : 2 * l + 1, :]
                first = turned[2 * l + 1 : 2 * l + 2, :]
                stage[2 + k, l : l + 1, 0:unit] = first
                stage[2 + nu + k, l : l + 1, 0:unit] = last
                pack[base + short + k, l : l + 1, 0:unit] = jnp.where(left, first, last)

    def send(s):
        pack, stage, halo = packs[s], stages[s], halos[s]

        def near(src, dst, size, where):
            pltpu.make_async_remote_copy(
                stage.at[pl.ds(src, size)], halo.at[pl.ds(dst, size)],
                halo_send.at[s], halo_recv.at[s], device_id=where, device_id_type=MESH,
            ).start()

        def far(size):
            def step(k, carry):
                d = lax.rem(me + k, ndev)
                mine = pack.at[pl.ds(base, size)]
                pltpu.make_async_remote_copy(
                    mine, mine, pack_send.at[s], pack_recv.at[s],
                    device_id=(lax.div(d, nc), lax.rem(d, nc)), device_id_type=MESH,
                ).start()
                return carry

            lax.fori_loop(1, ndev, step, 0)

        @pl.when(side)
        def _():
            far(full)

        @pl.when(jnp.logical_not(side))
        def _():
            far(short)

        near(0, 1, 1, (up, c))
        near(0, 5, 1, (up, west))
        near(0, 4, 1, (up, east))
        near(1, 0, 1, (down, c))
        near(1, 3, 1, (down, west))
        near(1, 2, 1, (down, east))
        near(2, 6 + nu, nu, (i, west))
        near(2 + nu, 6, nu, (i, east))

    everything = 2 * nr * full + (nc - 2) * nr * short

    def pack_wait(s, sem, side_units, mid_units):
        pack = packs[s]

        def take(units):
            part = pack.at[pl.ds(0, units)]
            pltpu.make_async_copy(part, part, sem.at[s]).wait()

        @pl.when(side)
        def _():
            take(side_units)

        @pl.when(jnp.logical_not(side))
        def _():
            take(mid_units)

    def receive(s):
        halo = halos[s]
        pltpu.make_async_copy(halo, halo, halo_recv.at[s]).wait()
        pack_wait(s, pack_recv, everything - full, everything - short)

    def finish(s):
        halo = halos[s]
        pltpu.make_async_copy(halo, halo, halo_send.at[s]).wait()
        pack_wait(s, pack_send, (ndev - 1) * full, (ndev - 1) * short)

    def triple(mid, before, after):
        mid, before, after = (
            jnp.concatenate([x, jnp.zeros((8 - x.shape[0], LANES), jnp.float32)], axis=0)
            for x in (mid, before, after)
        )
        west_of = jnp.where(small_lane == 0, before, pltpu.roll(mid, 1, 1))
        east_of = jnp.where(
            small_lane == LANES - 1, pltpu.roll(after, LANES - 1, 1), pltpu.roll(mid, LANES - 1, 1)
        )
        return mid + west_of + east_of

    def sweep(s, dest):
        pack, halo = packs[s], halos[s]
        for n, (at, _) in enumerate(items):
            picked[n * levels : (n + 1) * levels, :] = pack[at]
        raw = picked[...]
        picked[...] = jnp.where(flags[...] == 1, jnp.take_along_axis(raw, turn, axis=1), raw)

        def item(n):
            return picked[n * levels : (n + 1) * levels, :]

        def whole_line(n):
            if nw == 1:
                return item(n)
            return jnp.concatenate([item(n + k)[:, 0:unit] for k in range(nw)], axis=1)

        for k in range(nu):
            own = item(side0 + k)
            at = k * 2 * levels
            cols[at : at + levels, :] = jnp.where(left, own, halo[6 + k])
            cols[at + levels : at + 2 * levels, :] = jnp.where(right, own, halo[6 + nu + k])
        columns = cols[...].T

        ghost_top = triple(whole_line(top0), item(top0 + nw), item(top0 + nw + 1))
        ghost_bottom = triple(whole_line(bottom0), item(bottom0 + nw), item(bottom0 + nw + 1))

        def end_of(x):
            return jnp.concatenate([x[:, LANES - 1 :], x[:, : LANES - 1]], axis=1)

        above = triple(
            halo[0],
            jnp.where(left, item(up_cell), end_of(halo[2])),
            jnp.where(right, item(up_cell), halo[3]),
        )
        below = triple(
            halo[1],
            jnp.where(left, item(down_cell), end_of(halo[4])),
            jnp.where(right, item(down_cell), halo[5]),
        )
        for l in range(levels):
            hsum[l, 7:8, :] = above[l : l + 1]
            hsum[l, 8 + rows : 9 + rows, :] = below[l : l + 1]
            for k in range(nu):
                x = field[l, k * unit : (k + 1) * unit, :]
                j = k * 2 * levels + l
                w = columns[0:unit, j : j + 1]
                e = columns[0:unit, j + levels : j + levels + 1]
                west_of = jnp.where(lane == 0, w, pltpu.roll(x, 1, 1))
                east_of = jnp.where(lane == LANES - 1, e, pltpu.roll(x, LANES - 1, 1))
                hsum[l, 8 + k * unit : 8 + (k + 1) * unit, :] = x + west_of + east_of
        for l in range(levels):
            for k in range(nu):
                r0 = k * unit
                x = field[l, r0 : r0 + unit, :]
                upper = jnp.where(
                    local_row == top_hit - r0, ghost_top[l : l + 1], hsum[l, 7 + r0 : 7 + r0 + unit, :]
                )
                lower = jnp.where(
                    local_row == bottom_hit - r0,
                    ghost_bottom[l : l + 1],
                    hsum[l, 9 + r0 : 9 + r0 + unit, :],
                )
                box = upper + hsum[l, 8 + r0 : 8 + r0 + unit, :] + lower
                dest[l, r0 : r0 + unit, :] = x + rate[r0 : r0 + unit, :] * (box - 9.0 * x)

    loads[0].wait()
    prepare(0)
    loads[1].wait()
    loads[2].wait()
    rate[...] = rate[...] * area[...] * 0.125
    pl.semaphore_wait(barrier, ndev - 1)
    for s in range(SWEEPS):
        send(s)
        receive(s)
        sweep(s, out if s == SWEEPS - 1 else field)
        if s < SWEEPS - 1:
            prepare(s + 1)
    for s in range(SWEEPS):
        finish(s)


def on_device(noise, kappa, metric, edge_src, edge_rev, corner_src):
    levels, rows, width = noise.shape
    nr, nc = lax.axis_size("row"), lax.axis_size("col")
    unit = math.gcd(math.gcd(rows, width * nc // 2), width)
    nu, nw = rows // unit, width // unit
    count = 2 * (nw + 2) + nu + 2
    picked_rows = -(-count * levels // 8) * 8
    col_rows = -(-nu * 2 * levels // 8) * 8
    full = 2 * nw + nu
    scratch = [
        pltpu.VMEM((levels, rows, width), jnp.float32),
        pltpu.VMEM((rows, width), jnp.float32),
        pltpu.VMEM((rows, width), jnp.float32),
        pltpu.VMEM((levels, rows + 16, width), jnp.float32),
        pltpu.VMEM((picked_rows, LANES), jnp.float32),
        pltpu.VMEM((picked_rows, LANES), jnp.int32),
        pltpu.VMEM((col_rows, LANES), jnp.float32),
    ]
    scratch += [pltpu.VMEM((nr * nc * full, levels, LANES), jnp.float32)] * SWEEPS
    scratch += [pltpu.VMEM((2 + 2 * nu, levels, LANES), jnp.float32)] * SWEEPS
    scratch += [pltpu.VMEM((6 + 2 * nu, levels, LANES), jnp.float32)] * SWEEPS
    scratch += [pltpu.SemaphoreType.DMA((3,))]
    scratch += [pltpu.SemaphoreType.DMA((SWEEPS,))] * 4
    anywhere = pl.BlockSpec(memory_space=pl.ANY)
    small = pl.BlockSpec(memory_space=pltpu.SMEM)
    return pl.pallas_call(
        functools.partial(kernel, (levels, rows, width, nr, nc)),
        out_shape=jax.ShapeDtypeStruct(noise.shape, jnp.float32),
        in_specs=[anywhere] * 3 + [small] * 3,
        out_specs=pl.BlockSpec(memory_space=pltpu.VMEM),
        scratch_shapes=scratch,
        compiler_params=pltpu.CompilerParams(
            collective_id=0, has_side_effects=True, vmem_limit_bytes=48 * 1024 * 1024
        ),
    )(noise, kappa, metric, edge_src, edge_rev, corner_src)


def solution(mesh):
    in_specs = (P(None, "row", "col"), P("row", "col"), P("row", "col"), P(), P(), P())
    out_specs = P(None, "row", "col")
    return jax.shard_map(
        on_device, mesh=mesh, in_specs=in_specs, out_specs=out_specs, check_vma=False
    )
```

```python
import functools
import math

import jax
import jax.numpy as jnp
from jax import lax
from jax.experimental import pallas as pl
from jax.experimental.pallas import tpu as pltpu
from jax.sharding import PartitionSpec as P

SWEEPS = 4
LANES = 128
MESH = pl.DeviceIdType.MESH


def kernel(
    dims, noise, kappa, metric, esrc_in, erev_in, csrc_in, out,
    field, rate, area, hsum, picked, flags, cols, *rest
):
    levels, rows, width, nr, nc = dims
    packs, stages, halos = rest[0:4], rest[4:8], rest[8:12]
    in_sem, pack_send, pack_recv, halo_send, halo_recv, esrc, erev, csrc = rest[12:20]
    ndev = nr * nc
    face = width * nc
    total = 6 * face
    offset = face // 2
    unit = math.gcd(math.gcd(rows, offset), width)
    nu = rows // unit
    nw = width // unit
    per_face = face // unit
    short, full = 2 * nw, 2 * nw + nu

    i = lax.axis_index("row")
    c = lax.axis_index("col")
    me = i * nc + c
    left = c == 0
    right = c == nc - 1
    side = jnp.logical_or(left, right)

    loads = [
        pltpu.make_async_copy(noise, field, in_sem.at[0]),
        pltpu.make_async_copy(kappa, rate, in_sem.at[1]),
        pltpu.make_async_copy(metric, area, in_sem.at[2]),
        pltpu.make_async_copy(esrc_in, esrc, in_sem.at[3]),
        pltpu.make_async_copy(erev_in, erev, in_sem.at[4]),
        pltpu.make_async_copy(csrc_in, csrc, in_sem.at[5]),
    ]
    for load in loads:
        load.start()

    barrier = pltpu.get_barrier_semaphore()

    def greet(k, carry):
        d = lax.rem(me + k, ndev)
        pl.semaphore_signal(
            barrier, inc=1, device_id=(lax.div(d, nc), lax.rem(d, nc)), device_id_type=MESH
        )
        return carry

    lax.fori_loop(1, ndev, greet, 0)

    for load in loads[3:]:
        load.wait()

    start = lax.rem(i * rows + offset, total)
    f0 = lax.div(start, face)
    into = start - f0 * face
    has_top = jnp.logical_or(into == 0, into + rows > face)
    has_bottom = into + rows >= face
    top_face = jnp.where(into == 0, f0, lax.rem(f0 + 1, 6))
    top_row = jnp.where(into == 0, 0, face - into)
    bottom_row = face - 1 - into
    top_at = jnp.where(has_top, top_row, 0)
    bottom_at = jnp.where(has_bottom, bottom_row, 0)
    top_hit = jnp.where(has_top, top_row, -1)
    bottom_hit = jnp.where(has_bottom, bottom_row, -1)

    def place(line, u):
        f = lax.div(line, 4)
        e = lax.rem(line, 4)
        row_stored = lax.rem(f * face + jnp.where(e == 1, face - 1, 0) + total - offset, total)
        row_at = (lax.div(row_stored, rows) * nc + lax.div(u, nw)) * full + e * nw + lax.rem(u, nw)
        side_stored = lax.rem(f * face + u * unit + total - offset, total)
        d = lax.div(side_stored, rows)
        k = lax.div(side_stored - d * rows, unit)
        side_at = (d * nc + jnp.where(e == 3, nc - 1, 0)) * full + short + k
        return jnp.where(e < 2, row_at, side_at)

    def ghost_unit(edge, u):
        turned = erev[edge]
        return place(esrc[edge], jnp.where(turned == 1, per_face - 1 - u, u)), turned

    def corner(index):
        s = csrc[index]
        end = lax.rem(s, 2)
        return place(lax.div(s, 2), end * (per_face - 1)), end

    def ghost_cell(edge, u, end):
        turned = erev[edge]
        at = place(esrc[edge], jnp.where(turned == 1, per_face - 1 - u, u))
        return at, jnp.where(turned == 1, 1 - end, end)

    def choose(flag, a, b):
        return jnp.where(flag, a[0], b[0]), jnp.where(flag, a[1], b[1])

    items = []
    bottom_face = f0
    for f, e, q0 in ((top_face, 0, 0), (bottom_face, 1, 2)):
        edge = 4 * f + e
        for k in range(nw):
            items.append(ghost_unit(edge, c * nw + k))
        before = ghost_cell(edge, jnp.maximum(c * nw - 1, 0), 1)
        after = ghost_cell(edge, jnp.minimum(c * nw + nw, per_face - 1), 0)
        items.append(choose(left, corner(4 * f + q0), before))
        items.append(choose(right, corner(4 * f + q0 + 1), after))
    side_edge = jnp.where(left, 2, 3)
    for k in range(nu):
        at = lax.rem(start + k * unit, total)
        f = lax.div(at, face)
        items.append(ghost_unit(4 * f + side_edge, lax.div(at - f * face, unit)))
    at = lax.rem(start + total - unit, total)
    f = lax.div(at, face)
    items.append(ghost_cell(4 * f + side_edge, lax.div(at - f * face, unit), 1))
    at = lax.rem(start + rows, total)
    f = lax.div(at, face)
    items.append(ghost_cell(4 * f + side_edge, lax.div(at - f * face, unit), 0))
    top0, bottom0, side0 = 0, nw + 2, 2 * (nw + 2)
    up_cell, down_cell = side0 + nu, side0 + nu + 1
    for n, (_, flip) in enumerate(items):
        flags[n * levels : (n + 1) * levels, :] = jnp.full((levels, LANES), flip, jnp.int32)

    lane = lax.broadcasted_iota(jnp.int32, (unit, LANES), 1)
    local_row = lax.broadcasted_iota(jnp.int32, (unit, LANES), 0)
    small_lane = lax.broadcasted_iota(jnp.int32, (8, LANES), 1)
    turn = lax.rem(
        unit - 1 - lax.broadcasted_iota(jnp.int32, (picked.shape[0], LANES), 1) + LANES, LANES
    )

    base = me * full
    up = lax.rem(i + nr - 1, nr)
    down = lax.rem(i + 1, nr)
    west = lax.rem(c + nc - 1, nc)
    east = lax.rem(c + 1, nc)

    def prepare(s):
        pack, stage = packs[s], stages[s]
        for l in range(levels):
            stage[0, l : l + 1, :] = field[l, 0:1, :]
            stage[1, l : l + 1, :] = field[l, rows - 1 : rows, :]
            for e, row in ((0, top_at), (1, bottom_at)):
                line = field[l, pl.ds(row, 1), :]
                for k in range(nw):
                    part = line if k == 0 else jnp.roll(line, -k * unit, axis=1)
                    pack[base + e * nw + k, l : l + 1, :] = part
        for k in range(nu):
            both = jnp.zeros((unit, LANES), jnp.float32)
            for l in range(levels):
                block = field[l, k * unit : (k + 1) * unit, :]
                both = jnp.where(lane >= 2 * l, pltpu.roll(block, 1 + 2 * l, 1), both)
            turned = both.T
            for l in range(levels):
                last = turned[2 * l : 2 * l + 1, :]
                first = turned[2 * l + 1 : 2 * l + 2, :]
                stage[2 + k, l : l + 1, 0:unit] = first
                stage[2 + nu + k, l : l + 1, 0:unit] = last
                pack[base + short + k, l : l + 1, 0:unit] = jnp.where(left, first, last)

    def send(s):
        pack, stage, halo = packs[s], stages[s], halos[s]

        def near(src, dst, size, where):
            pltpu.make_async_remote_copy(
                stage.at[pl.ds(src, size)], halo.at[pl.ds(dst, size)],
                halo_send.at[s], halo_recv.at[s], device_id=where, device_id_type=MESH,
            ).start()

        def far(size):
            def step(k, carry):
                d = lax.rem(me + k, ndev)
                mine = pack.at[pl.ds(base, size)]
                pltpu.make_async_remote_copy(
                    mine, mine, pack_send.at[s], pack_recv.at[s],
                    device_id=(lax.div(d, nc), lax.rem(d, nc)), device_id_type=MESH,
                ).start()
                return carry

            lax.fori_loop(1, ndev, step, 0)

        near(0, 1, 1, (up, c))
        near(0, 5, 1, (up, west))
        near(0, 4, 1, (up, east))
        near(1, 0, 1, (down, c))
        near(1, 3, 1, (down, west))
        near(1, 2, 1, (down, east))
        near(2, 6 + nu, nu, (i, west))
        near(2 + nu, 6, nu, (i, east))

        @pl.when(side)
        def _():
            far(full)

        @pl.when(jnp.logical_not(side))
        def _():
            far(short)

    everything = 2 * nr * full + (nc - 2) * nr * short

    def pack_wait(s, sem, side_units, mid_units):
        pack = packs[s]

        def take(units):
            part = pack.at[pl.ds(0, units)]
            pltpu.make_async_copy(part, part, sem.at[s]).wait()

        @pl.when(side)
        def _():
            take(side_units)

        @pl.when(jnp.logical_not(side))
        def _():
            take(mid_units)

    def receive(s):
        halo = halos[s]
        pltpu.make_async_copy(halo, halo, halo_recv.at[s]).wait()
        pack_wait(s, pack_recv, everything - full, everything - short)

    def finish(s):
        halo = halos[s]
        pltpu.make_async_copy(halo, halo, halo_send.at[s]).wait()
        pack_wait(s, pack_send, (ndev - 1) * full, (ndev - 1) * short)

    def triple(mid, before, after):
        mid, before, after = (
            jnp.concatenate([x, jnp.zeros((8 - x.shape[0], LANES), jnp.float32)], axis=0)
            for x in (mid, before, after)
        )
        west_of = jnp.where(small_lane == 0, before, pltpu.roll(mid, 1, 1))
        east_of = jnp.where(
            small_lane == LANES - 1, pltpu.roll(after, LANES - 1, 1), pltpu.roll(mid, LANES - 1, 1)
        )
        return mid + west_of + east_of

    def sweep(s, dest):
        pack, halo = packs[s], halos[s]
        for n, (at, _) in enumerate(items):
            picked[n * levels : (n + 1) * levels, :] = pack[at]
        raw = picked[...]
        picked[...] = jnp.where(flags[...] == 1, jnp.take_along_axis(raw, turn, axis=1), raw)

        def item(n):
            return picked[n * levels : (n + 1) * levels, :]

        def whole_line(n):
            if nw == 1:
                return item(n)
            return jnp.concatenate([item(n + k)[:, 0:unit] for k in range(nw)], axis=1)

        for k in range(nu):
            own = item(side0 + k)
            at = k * 2 * levels
            cols[at : at + levels, :] = jnp.where(left, own, halo[6 + k])
            cols[at + levels : at + 2 * levels, :] = jnp.where(right, own, halo[6 + nu + k])
        columns = cols[...].T

        ghost_top = triple(whole_line(top0), item(top0 + nw), item(top0 + nw + 1))
        ghost_bottom = triple(whole_line(bottom0), item(bottom0 + nw), item(bottom0 + nw + 1))

        def end_of(x):
            return jnp.concatenate([x[:, LANES - 1 :], x[:, : LANES - 1]], axis=1)

        above = triple(
            halo[0],
            jnp.where(left, item(up_cell), end_of(halo[2])),
            jnp.where(right, item(up_cell), halo[3]),
        )
        below = triple(
            halo[1],
            jnp.where(left, item(down_cell), end_of(halo[4])),
            jnp.where(right, item(down_cell), halo[5]),
        )
        for l in range(levels):
            hsum[l, 7:8, :] = above[l : l + 1]
            hsum[l, 8 + rows : 9 + rows, :] = below[l : l + 1]
            for k in range(nu):
                x = field[l, k * unit : (k + 1) * unit, :]
                j = k * 2 * levels + l
                w = columns[0:unit, j : j + 1]
                e = columns[0:unit, j + levels : j + levels + 1]
                west_of = jnp.where(lane == 0, w, pltpu.roll(x, 1, 1))
                east_of = jnp.where(lane == LANES - 1, e, pltpu.roll(x, LANES - 1, 1))
                hsum[l, 8 + k * unit : 8 + (k + 1) * unit, :] = x + west_of + east_of
        for l in range(levels):
            for k in range(nu):
                r0 = k * unit
                x = field[l, r0 : r0 + unit, :]
                upper = jnp.where(
                    local_row == top_hit - r0, ghost_top[l : l + 1], hsum[l, 7 + r0 : 7 + r0 + unit, :]
                )
                lower = jnp.where(
                    local_row == bottom_hit - r0,
                    ghost_bottom[l : l + 1],
                    hsum[l, 9 + r0 : 9 + r0 + unit, :],
                )
                box = upper + hsum[l, 8 + r0 : 8 + r0 + unit, :] + lower
                dest[l, r0 : r0 + unit, :] = x + rate[r0 : r0 + unit, :] * (box - 9.0 * x)

    loads[0].wait()
    prepare(0)
    loads[1].wait()
    loads[2].wait()
    rate[...] = rate[...] * area[...] * 0.125
    pl.semaphore_wait(barrier, ndev - 1)
    for s in range(SWEEPS):
        send(s)
        receive(s)
        sweep(s, out if s == SWEEPS - 1 else field)
        if s < SWEEPS - 1:
            prepare(s + 1)
    for s in range(SWEEPS):
        finish(s)


def on_device(noise, kappa, metric, edge_src, edge_rev, corner_src):
    levels, rows, width = noise.shape
    nr, nc = lax.axis_size("row"), lax.axis_size("col")
    unit = math.gcd(math.gcd(rows, width * nc // 2), width)
    nu, nw = rows // unit, width // unit
    count = 2 * (nw + 2) + nu + 2
    picked_rows = -(-count * levels // 8) * 8
    col_rows = -(-nu * 2 * levels // 8) * 8
    full = 2 * nw + nu
    scratch = [
        pltpu.VMEM((levels, rows, width), jnp.float32),
        pltpu.VMEM((rows, width), jnp.float32),
        pltpu.VMEM((rows, width), jnp.float32),
        pltpu.VMEM((levels, rows + 16, width), jnp.float32),
        pltpu.VMEM((picked_rows, LANES), jnp.float32),
        pltpu.VMEM((picked_rows, LANES), jnp.int32),
        pltpu.VMEM((col_rows, LANES), jnp.float32),
    ]
    scratch += [pltpu.VMEM((nr * nc * full, levels, LANES), jnp.float32)] * SWEEPS
    scratch += [pltpu.VMEM((2 + 2 * nu, levels, LANES), jnp.float32)] * SWEEPS
    scratch += [pltpu.VMEM((6 + 2 * nu, levels, LANES), jnp.float32)] * SWEEPS
    scratch += [pltpu.SemaphoreType.DMA((6,))]
    scratch += [pltpu.SemaphoreType.DMA((SWEEPS,))] * 4
    scratch += [pltpu.SMEM(edge_src.shape, jnp.int32)] * 3
    in_hbm = pl.BlockSpec(memory_space=pltpu.HBM)
    return pl.pallas_call(
        functools.partial(kernel, (levels, rows, width, nr, nc)),
        out_shape=jax.ShapeDtypeStruct(noise.shape, jnp.float32),
        in_specs=[in_hbm] * 6,
        out_specs=pl.BlockSpec(memory_space=pltpu.VMEM),
        scratch_shapes=scratch,
        compiler_params=pltpu.CompilerParams(
            collective_id=0, has_side_effects=True, vmem_limit_bytes=48 * 1024 * 1024
        ),
    )(noise, kappa, metric, edge_src, edge_rev, corner_src)


def solution(mesh):
    in_specs = (P(None, "row", "col"), P("row", "col"), P("row", "col"), P(), P(), P())
    out_specs = P(None, "row", "col")
    return jax.shard_map(
        on_device, mesh=mesh, in_specs=in_specs, out_specs=out_specs, check_vma=False
    )
```

```python
import functools
import math

import jax
import jax.numpy as jnp
from jax import lax
from jax.experimental import pallas as pl
from jax.experimental.pallas import tpu as pltpu
from jax.sharding import PartitionSpec as P

SWEEPS = 4
LANES = 128
MESH = pl.DeviceIdType.MESH


def kernel(
    dims, noise, kappa, metric, esrc_in, erev_in, csrc_in, out,
    field, other, rate, area, hsum, picked, flags, *rest
):
    levels, rows, width, nr, nc = dims
    packs, stages, halos = rest[0:4], rest[4:8], rest[8:12]
    in_sem, pack_send, pack_recv, halo_send, halo_recv, esrc, erev, csrc = rest[12:20]
    ndev = nr * nc
    face = width * nc
    total = 6 * face
    offset = face // 2
    unit = math.gcd(math.gcd(rows, offset), width)
    nu = rows // unit
    nw = width // unit
    per_face = face // unit
    short, full = 2 * nw, 2 * nw + nu

    i = lax.axis_index("row")
    c = lax.axis_index("col")
    me = i * nc + c
    left = c == 0
    right = c == nc - 1
    side = jnp.logical_or(left, right)

    loads = [
        pltpu.make_async_copy(noise, field, in_sem.at[0]),
        pltpu.make_async_copy(kappa, rate, in_sem.at[1]),
        pltpu.make_async_copy(metric, area, in_sem.at[2]),
        pltpu.make_async_copy(esrc_in, esrc, in_sem.at[3]),
        pltpu.make_async_copy(erev_in, erev, in_sem.at[4]),
        pltpu.make_async_copy(csrc_in, csrc, in_sem.at[5]),
    ]
    for load in loads:
        load.start()

    barrier = pltpu.get_barrier_semaphore()

    def greet(k, carry):
        d = lax.rem(me + k, ndev)
        pl.semaphore_signal(
            barrier, inc=1, device_id=(lax.div(d, nc), lax.rem(d, nc)), device_id_type=MESH
        )
        return carry

    lax.fori_loop(1, ndev, greet, 0)

    for load in loads[3:]:
        load.wait()

    start = lax.rem(i * rows + offset, total)
    f0 = lax.div(start, face)
    into = start - f0 * face
    has_top = jnp.logical_or(into == 0, into + rows > face)
    has_bottom = into + rows >= face
    top_face = jnp.where(into == 0, f0, lax.rem(f0 + 1, 6))
    top_row = jnp.where(into == 0, 0, face - into)
    bottom_row = face - 1 - into
    top_at = jnp.where(has_top, top_row, 0)
    bottom_at = jnp.where(has_bottom, bottom_row, 0)
    top_hit = jnp.where(has_top, top_row, -1)
    bottom_hit = jnp.where(has_bottom, bottom_row, -1)

    def place(line, u):
        f = lax.div(line, 4)
        e = lax.rem(line, 4)
        row_stored = lax.rem(f * face + jnp.where(e == 1, face - 1, 0) + total - offset, total)
        row_at = (lax.div(row_stored, rows) * nc + lax.div(u, nw)) * full + e * nw + lax.rem(u, nw)
        side_stored = lax.rem(f * face + u * unit + total - offset, total)
        d = lax.div(side_stored, rows)
        k = lax.div(side_stored - d * rows, unit)
        side_at = (d * nc + jnp.where(e == 3, nc - 1, 0)) * full + short + k
        return jnp.where(e < 2, row_at, side_at)

    def ghost_unit(edge, u):
        turned = erev[edge]
        return place(esrc[edge], jnp.where(turned == 1, per_face - 1 - u, u)), turned

    def corner(index):
        s = csrc[index]
        end = lax.rem(s, 2)
        return place(lax.div(s, 2), end * (per_face - 1)), end

    def ghost_cell(edge, u, end):
        turned = erev[edge]
        at = place(esrc[edge], jnp.where(turned == 1, per_face - 1 - u, u))
        return at, jnp.where(turned == 1, 1 - end, end)

    def choose(flag, a, b):
        return jnp.where(flag, a[0], b[0]), jnp.where(flag, a[1], b[1])

    items = []
    bottom_face = f0
    for f, e, q0 in ((top_face, 0, 0), (bottom_face, 1, 2)):
        edge = 4 * f + e
        for k in range(nw):
            items.append(ghost_unit(edge, c * nw + k))
        before = ghost_cell(edge, jnp.maximum(c * nw - 1, 0), 1)
        after = ghost_cell(edge, jnp.minimum(c * nw + nw, per_face - 1), 0)
        items.append(choose(left, corner(4 * f + q0), before))
        items.append(choose(right, corner(4 * f + q0 + 1), after))
    side_edge = jnp.where(left, 2, 3)
    for k in range(nu):
        at = lax.rem(start + k * unit, total)
        f = lax.div(at, face)
        items.append(ghost_unit(4 * f + side_edge, lax.div(at - f * face, unit)))
    at = lax.rem(start + total - unit, total)
    f = lax.div(at, face)
    items.append(ghost_cell(4 * f + side_edge, lax.div(at - f * face, unit), 1))
    at = lax.rem(start + rows, total)
    f = lax.div(at, face)
    items.append(ghost_cell(4 * f + side_edge, lax.div(at - f * face, unit), 0))
    top0, bottom0, side0 = 0, nw + 2, 2 * (nw + 2)
    up_cell, down_cell = side0 + nu, side0 + nu + 1
    for n, (_, flip) in enumerate(items):
        flags[n * levels : (n + 1) * levels, :] = jnp.full((levels, LANES), flip, jnp.int32)

    lane = lax.broadcasted_iota(jnp.int32, (unit, LANES), 1)
    local_row = lax.broadcasted_iota(jnp.int32, (unit, LANES), 0)
    small_lane = lax.broadcasted_iota(jnp.int32, (8, LANES), 1)
    turn = lax.rem(
        unit - 1 - lax.broadcasted_iota(jnp.int32, (picked.shape[0], LANES), 1) + LANES, LANES
    )

    wide = (8, levels * LANES)
    goal = lax.broadcasted_iota(jnp.int32, wide, 1)
    source = lax.broadcasted_iota(jnp.int32, wide, 0)
    spread = jnp.zeros(wide, jnp.float32)
    for l in range(levels):
        spread = jnp.where(jnp.logical_and(source == l, goal == l * LANES), 1.0, spread)
        spread = jnp.where(
            jnp.logical_and(source == levels + l, goal == (l + 1) * LANES - 1), 1.0, spread
        )

    base = me * full
    up = lax.rem(i + nr - 1, nr)
    down = lax.rem(i + 1, nr)
    west = lax.rem(c + nc - 1, nc)
    east = lax.rem(c + 1, nc)

    def prepare(s, field):
        pack, stage = packs[s], stages[s]
        for l in range(levels):
            stage[0, l : l + 1, :] = field[l, 0:1, :]
            stage[1, l : l + 1, :] = field[l, rows - 1 : rows, :]
            for e, row in ((0, top_at), (1, bottom_at)):
                line = field[l, pl.ds(row, 1), :]
                for k in range(nw):
                    part = line if k == 0 else jnp.roll(line, -k * unit, axis=1)
                    pack[base + e * nw + k, l : l + 1, :] = part
        for k in range(nu):
            both = jnp.zeros((unit, LANES), jnp.float32)
            for l in range(levels):
                block = field[l, k * unit : (k + 1) * unit, :]
                both = jnp.where(lane >= 2 * l, pltpu.roll(block, 1 + 2 * l, 1), both)
            turned = both.T
            for l in range(levels):
                last = turned[2 * l : 2 * l + 1, :]
                first = turned[2 * l + 1 : 2 * l + 2, :]
                stage[2 + k, l : l + 1, 0:unit] = first
                stage[2 + nu + k, l : l + 1, 0:unit] = last
                pack[base + short + k, l : l + 1, 0:unit] = jnp.where(left, first, last)

    def send(s):
        pack, stage, halo = packs[s], stages[s], halos[s]

        def near(src, dst, size, where):
            pltpu.make_async_remote_copy(
                stage.at[pl.ds(src, size)], halo.at[pl.ds(dst, size)],
                halo_send.at[s], halo_recv.at[s], device_id=where, device_id_type=MESH,
            ).start()

        def far(size):
            def step(k, carry):
                d = lax.rem(me + k, ndev)
                mine = pack.at[pl.ds(base, size)]
                pltpu.make_async_remote_copy(
                    mine, mine, pack_send.at[s], pack_recv.at[s],
                    device_id=(lax.div(d, nc), lax.rem(d, nc)), device_id_type=MESH,
                ).start()
                return carry

            lax.fori_loop(1, ndev, step, 0)

        near(0, 1, 1, (up, c))
        near(0, 5, 1, (up, west))
        near(0, 4, 1, (up, east))
        near(1, 0, 1, (down, c))
        near(1, 3, 1, (down, west))
        near(1, 2, 1, (down, east))
        near(2, 6 + nu, nu, (i, west))
        near(2 + nu, 6, nu, (i, east))

        @pl.when(side)
        def _():
            far(full)

        @pl.when(jnp.logical_not(side))
        def _():
            far(short)

    everything = 2 * nr * full + (nc - 2) * nr * short

    def pack_wait(s, sem, side_units, mid_units):
        pack = packs[s]

        def take(units):
            part = pack.at[pl.ds(0, units)]
            pltpu.make_async_copy(part, part, sem.at[s]).wait()

        @pl.when(side)
        def _():
            take(side_units)

        @pl.when(jnp.logical_not(side))
        def _():
            take(mid_units)

    def receive(s):
        halo = halos[s]
        pltpu.make_async_copy(halo, halo, halo_recv.at[s]).wait()
        pack_wait(s, pack_recv, everything - full, everything - short)

    def finish(s):
        halo = halos[s]
        pltpu.make_async_copy(halo, halo, halo_send.at[s]).wait()
        pack_wait(s, pack_send, (ndev - 1) * full, (ndev - 1) * short)

    def triple(mid, before, after):
        mid, before, after = (
            jnp.concatenate([x, jnp.zeros((8 - x.shape[0], LANES), jnp.float32)], axis=0)
            for x in (mid, before, after)
        )
        west_of = jnp.where(small_lane == 0, before, pltpu.roll(mid, 1, 1))
        east_of = jnp.where(
            small_lane == LANES - 1, pltpu.roll(after, LANES - 1, 1), pltpu.roll(mid, LANES - 1, 1)
        )
        return mid + west_of + east_of

    def partial(src, dest):
        for l in range(levels):
            for k in range(nu):
                x = src[l, k * unit : (k + 1) * unit, :]
                west_of = jnp.where(lane == 0, 0.0, pltpu.roll(x, 1, 1))
                east_of = jnp.where(lane == LANES - 1, 0.0, pltpu.roll(x, LANES - 1, 1))
                hsum[l, 8 + k * unit : 8 + (k + 1) * unit, :] = x + west_of + east_of
        for l in range(levels):
            for k in range(nu):
                r0 = k * unit
                x = src[l, r0 : r0 + unit, :]
                upper = jnp.where(
                    local_row == top_hit - r0, 0.0, hsum[l, 7 + r0 : 7 + r0 + unit, :]
                )
                lower = jnp.where(
                    local_row == bottom_hit - r0, 0.0, hsum[l, 9 + r0 : 9 + r0 + unit, :]
                )
                box = upper + hsum[l, 8 + r0 : 8 + r0 + unit, :] + lower
                dest[l, r0 : r0 + unit, :] = x + rate[r0 : r0 + unit, :] * (box - 9.0 * x)

    def gather(s):
        pack, halo = packs[s], halos[s]
        for n, (at, _) in enumerate(items):
            picked[n * levels : (n + 1) * levels, :] = pack[at]
        raw = picked[...]
        picked[...] = jnp.where(flags[...] == 1, jnp.take_along_axis(raw, turn, axis=1), raw)

        def item(n):
            return picked[n * levels : (n + 1) * levels, :]

        def whole_line(n):
            if nw == 1:
                return item(n)
            return jnp.concatenate([item(n + k)[:, 0:unit] for k in range(nw)], axis=1)

        sides = []
        blank = jnp.zeros((8 - 2 * levels, LANES), jnp.float32)
        for k in range(nu):
            own = item(side0 + k)
            w = jnp.where(left, own, halo[6 + k])
            e = jnp.where(right, own, halo[6 + nu + k])
            both = jnp.concatenate([w, e, blank], axis=0)
            sides.append(both if unit == LANES else jnp.where(small_lane < unit, both, 0.0))
        nothing = jnp.zeros((8, LANES), jnp.float32)
        beside = []
        for k in range(nu):
            r0 = k * unit
            before = sides[k - 1] if k else nothing
            after = sides[k + 1] if k < nu - 1 else nothing
            prev = jnp.where(
                small_lane == 0,
                pltpu.roll(before, (LANES + 1 - unit) % LANES, 1),
                pltpu.roll(sides[k], 1, 1),
            )
            follow = jnp.where(
                small_lane == unit - 1,
                pltpu.roll(after, unit - 1, 1),
                pltpu.roll(sides[k], LANES - 1, 1),
            )
            prev = jnp.where(small_lane == top_hit - r0, 0.0, prev)
            follow = jnp.where(small_lane == bottom_hit - r0, 0.0, follow)
            sums = sides[k] + prev + follow
            beside.append(sums if unit == LANES else jnp.where(small_lane < unit, sums, 0.0))

        ghost_top = triple(whole_line(top0), item(top0 + nw), item(top0 + nw + 1))
        ghost_bottom = triple(whole_line(bottom0), item(bottom0 + nw), item(bottom0 + nw + 1))

        def end_of(x):
            return jnp.concatenate([x[:, LANES - 1 :], x[:, : LANES - 1]], axis=1)

        above = triple(
            halo[0],
            jnp.where(left, item(up_cell), end_of(halo[2])),
            jnp.where(right, item(up_cell), halo[3]),
        )
        below = triple(
            halo[1],
            jnp.where(left, item(down_cell), end_of(halo[4])),
            jnp.where(right, item(down_cell), halo[5]),
        )
        return beside, (
            (0, top_hit != 0, above),
            (rows - 1, bottom_hit != rows - 1, below),
            (top_at, has_top, ghost_top),
            (bottom_at, has_bottom, ghost_bottom),
        )

    def complete(dest, found):
        beside, lines = found
        for k in range(nu):
            r0 = k * unit
            extra = lax.dot_general(
                beside[k].T, spread, (((1,), (0,)), ((), ())),
                precision=lax.Precision.HIGHEST, preferred_element_type=jnp.float32,
            )[0:unit]
            scale = rate[r0 : r0 + unit, :]
            for l in range(levels):
                dest[l, r0 : r0 + unit, :] += scale * extra[:, l * LANES : (l + 1) * LANES]
        for row, used, h in lines:
            scale = rate[pl.ds(row, 1), :]
            for l in range(levels):
                more = jnp.where(used, scale * h[l : l + 1], 0.0)
                dest[l, pl.ds(row, 1), :] = dest[l, pl.ds(row, 1), :] + more

    def edge_columns(blocks_of):
        made = []
        for k in range(nu):
            both = jnp.zeros((unit, LANES), jnp.float32)
            for l in range(levels):
                block = blocks_of(l, k)
                first = block if l == 0 else pltpu.roll(block, l, 1)
                both = jnp.where(lane == l, first, both)
                both = jnp.where(lane == levels + l, pltpu.roll(block, levels + l + 1, 1), both)
            turned = both.T[0:8]
            if unit < LANES:
                blank = jnp.zeros((8, LANES - unit), jnp.float32)
                turned = jnp.concatenate([turned, blank], axis=1)
            made.append(turned)
        return made

    def prepare_next(s, dest, found, columns):
        beside, lines = found
        pack, stage = packs[s], stages[s]
        rank = lax.broadcasted_iota(jnp.int32, (8, LANES), 0)
        ends = []
        for row, used, h in lines:
            twice = h + pltpu.roll(h, levels, 0)
            at_end = small_lane == jnp.where(rank < levels, 0, LANES - 1)
            ends.append(jnp.sum(jnp.where(at_end, twice, 0.0), axis=1, keepdims=True))
        for k in range(nu):
            total_add = beside[k]
            for (row, used, _), end in zip(lines, ends):
                at = jnp.where(used, row - k * unit, -1)
                hit = small_lane == at
                if unit < LANES:
                    hit = jnp.logical_and(hit, small_lane < unit)
                total_add = total_add + jnp.where(hit, end, 0.0)
            fresh = columns[k] + rate_columns[k] * total_add
            first, last = fresh[0:levels], fresh[levels : 2 * levels]
            stage[2 + k] = first
            stage[2 + nu + k] = last
            pack[base + short + k] = jnp.where(left, first, last)
        for n, (row, _, _) in enumerate(lines):
            near_cells = jnp.zeros((8, LANES), jnp.float32)
            for k in range(nu):
                near_cells = near_cells + jnp.where(small_lane == row - k * unit, beside[k], 0.0)
            cells = jnp.sum(near_cells, axis=1, keepdims=True) + jnp.zeros((8, LANES), jnp.float32)
            more = jnp.where(small_lane == 0, cells, 0.0) + jnp.where(
                small_lane == LANES - 1, pltpu.roll(cells, 8 - levels, 0), 0.0
            )
            for other_row, used, h in lines:
                more = more + jnp.where(jnp.logical_and(used, other_row == row), h, 0.0)
            scale = rate[pl.ds(row, 1), :]
            for l in range(levels):
                line = dest[l, pl.ds(row, 1), :] + scale * more[l : l + 1]
                if n < 2:
                    stage[n, l : l + 1, :] = line
                else:
                    for k in range(nw):
                        part = line if k == 0 else jnp.roll(line, -k * unit, axis=1)
                        pack[base + (n - 2) * nw + k, l : l + 1, :] = part

    loads[0].wait()
    prepare(0, field)
    loads[1].wait()
    loads[2].wait()
    rate[...] = rate[...] * area[...] * 0.125
    pl.semaphore_wait(barrier, ndev - 1)
    for l in range(levels):
        hsum[l, 7:8, :] = jnp.zeros((1, LANES), jnp.float32)
        hsum[l, 8 + rows : 9 + rows, :] = jnp.zeros((1, LANES), jnp.float32)
    src, found = field, None
    for s in range(SWEEPS):
        final = s == SWEEPS - 1
        dest = out if final else (other if src is field else field)
        send(s)
        if s == 0:
            rate_columns = edge_columns(lambda l, k: rate[k * unit : (k + 1) * unit, :])
        else:
            complete(src, found)
        partial(src, dest)
        if not final:
            columns = edge_columns(lambda l, k: dest[l, k * unit : (k + 1) * unit, :])
        receive(s)
        found = gather(s)
        if final:
            complete(dest, found)
        else:
            prepare_next(s + 1, dest, found, columns)
        src = dest
    for s in range(SWEEPS):
        finish(s)


def on_device(noise, kappa, metric, edge_src, edge_rev, corner_src):
    levels, rows, width = noise.shape
    nr, nc = lax.axis_size("row"), lax.axis_size("col")
    unit = math.gcd(math.gcd(rows, width * nc // 2), width)
    nu, nw = rows // unit, width // unit
    count = 2 * (nw + 2) + nu + 2
    picked_rows = -(-count * levels // 8) * 8
    full = 2 * nw + nu
    scratch = [
        pltpu.VMEM((levels, rows, width), jnp.float32),
        pltpu.VMEM((levels, rows, width), jnp.float32),
        pltpu.VMEM((rows, width), jnp.float32),
        pltpu.VMEM((rows, width), jnp.float32),
        pltpu.VMEM((levels, rows + 16, width), jnp.float32),
        pltpu.VMEM((picked_rows, LANES), jnp.float32),
        pltpu.VMEM((picked_rows, LANES), jnp.int32),
    ]
    scratch += [pltpu.VMEM((nr * nc * full, levels, LANES), jnp.float32)] * SWEEPS
    scratch += [pltpu.VMEM((2 + 2 * nu, levels, LANES), jnp.float32)] * SWEEPS
    scratch += [pltpu.VMEM((6 + 2 * nu, levels, LANES), jnp.float32)] * SWEEPS
    scratch += [pltpu.SemaphoreType.DMA((6,))]
    scratch += [pltpu.SemaphoreType.DMA((SWEEPS,))] * 4
    scratch += [pltpu.SMEM(edge_src.shape, jnp.int32)] * 3
    in_hbm = pl.BlockSpec(memory_space=pltpu.HBM)
    return pl.pallas_call(
        functools.partial(kernel, (levels, rows, width, nr, nc)),
        out_shape=jax.ShapeDtypeStruct(noise.shape, jnp.float32),
        in_specs=[in_hbm] * 6,
        out_specs=pl.BlockSpec(memory_space=pltpu.VMEM),
        scratch_shapes=scratch,
        compiler_params=pltpu.CompilerParams(
            collective_id=0, has_side_effects=True, vmem_limit_bytes=48 * 1024 * 1024
        ),
    )(noise, kappa, metric, edge_src, edge_rev, corner_src)


def solution(mesh):
    in_specs = (P(None, "row", "col"), P("row", "col"), P("row", "col"), P(), P(), P())
    out_specs = P(None, "row", "col")
    return jax.shard_map(
        on_device, mesh=mesh, in_specs=in_specs, out_specs=out_specs, check_vma=False
    )
```

```python
import functools
import math

import jax
import jax.numpy as jnp
from jax import lax
from jax.experimental import pallas as pl
from jax.experimental.pallas import tpu as pltpu
from jax.sharding import PartitionSpec as P

SWEEPS = 4
LANES = 128
MESH = pl.DeviceIdType.MESH


def kernel(
    dims, noise, kappa, metric, esrc_in, erev_in, csrc_in, out,
    field, other, rate, area, hsum, picked, flags, *rest
):
    levels, rows, width, nr, nc = dims
    packs, stages, halos = rest[0:4], rest[4:8], rest[8:12]
    in_sem, pack_send, pack_recv, halo_send, halo_recv, esrc, erev, csrc = rest[12:20]
    ndev = nr * nc
    face = width * nc
    total = 6 * face
    offset = face // 2
    unit = math.gcd(math.gcd(rows, offset), width)
    nu = rows // unit
    nw = width // unit
    per_face = face // unit
    full = 2 * nw + nu

    i = lax.axis_index("row")
    c = lax.axis_index("col")
    me = i * nc + c
    left = c == 0
    right = c == nc - 1
    side = jnp.logical_or(left, right)

    loads = [
        pltpu.make_async_copy(noise, field, in_sem.at[0]),
        pltpu.make_async_copy(kappa, rate, in_sem.at[1]),
        pltpu.make_async_copy(metric, area, in_sem.at[2]),
        pltpu.make_async_copy(esrc_in, esrc, in_sem.at[3]),
        pltpu.make_async_copy(erev_in, erev, in_sem.at[4]),
        pltpu.make_async_copy(csrc_in, csrc, in_sem.at[5]),
    ]
    for load in loads:
        load.start()

    barrier = pltpu.get_barrier_semaphore()

    def greet(k, carry):
        d = lax.rem(me + k, ndev)
        pl.semaphore_signal(
            barrier, inc=1, device_id=(lax.div(d, nc), lax.rem(d, nc)), device_id_type=MESH
        )
        return carry

    lax.fori_loop(1, ndev, greet, 0)

    for load in loads[3:]:
        load.wait()

    start = lax.rem(i * rows + offset, total)
    f0 = lax.div(start, face)
    into = start - f0 * face
    has_top = jnp.logical_or(into == 0, into + rows > face)
    has_bottom = into + rows >= face
    top_face = jnp.where(into == 0, f0, lax.rem(f0 + 1, 6))
    top_row = jnp.where(into == 0, 0, face - into)
    bottom_row = face - 1 - into
    top_at = jnp.where(has_top, top_row, 0)
    bottom_at = jnp.where(has_bottom, bottom_row, 0)
    top_hit = jnp.where(has_top, top_row, -1)
    bottom_hit = jnp.where(has_bottom, bottom_row, -1)

    def two_lines(row):
        return lax.rem(row * rows + offset, face) + rows > face

    both_lines = two_lines(i)
    side_from = jnp.where(both_lines, 2 * nw, nw)

    def place(line, u):
        f = lax.div(line, 4)
        e = lax.rem(line, 4)
        row_stored = lax.rem(f * face + jnp.where(e == 1, face - 1, 0) + total - offset, total)
        owner = lax.div(row_stored, rows)
        slot = jnp.where(two_lines(owner), e * nw, 0)
        row_at = (owner * nc + lax.div(u, nw)) * full + slot + lax.rem(u, nw)
        side_stored = lax.rem(f * face + u * unit + total - offset, total)
        d = lax.div(side_stored, rows)
        k = lax.div(side_stored - d * rows, unit)
        side_at = (d * nc + jnp.where(e == 3, nc - 1, 0)) * full + jnp.where(two_lines(d), 2 * nw, nw) + k
        return jnp.where(e < 2, row_at, side_at)

    def ghost_unit(edge, u):
        turned = erev[edge]
        return place(esrc[edge], jnp.where(turned == 1, per_face - 1 - u, u)), turned

    def corner(index):
        s = csrc[index]
        end = lax.rem(s, 2)
        return place(lax.div(s, 2), end * (per_face - 1)), end

    def ghost_cell(edge, u, end):
        turned = erev[edge]
        at = place(esrc[edge], jnp.where(turned == 1, per_face - 1 - u, u))
        return at, jnp.where(turned == 1, 1 - end, end)

    def choose(flag, a, b):
        return jnp.where(flag, a[0], b[0]), jnp.where(flag, a[1], b[1])

    items = []
    bottom_face = f0
    for f, e, q0 in ((top_face, 0, 0), (bottom_face, 1, 2)):
        edge = 4 * f + e
        for k in range(nw):
            items.append(ghost_unit(edge, c * nw + k))
        before = ghost_cell(edge, jnp.maximum(c * nw - 1, 0), 1)
        after = ghost_cell(edge, jnp.minimum(c * nw + nw, per_face - 1), 0)
        items.append(choose(left, corner(4 * f + q0), before))
        items.append(choose(right, corner(4 * f + q0 + 1), after))
    side_edge = jnp.where(left, 2, 3)
    for k in range(nu):
        at = lax.rem(start + k * unit, total)
        f = lax.div(at, face)
        items.append(ghost_unit(4 * f + side_edge, lax.div(at - f * face, unit)))
    at = lax.rem(start + total - unit, total)
    f = lax.div(at, face)
    items.append(ghost_cell(4 * f + side_edge, lax.div(at - f * face, unit), 1))
    at = lax.rem(start + rows, total)
    f = lax.div(at, face)
    items.append(ghost_cell(4 * f + side_edge, lax.div(at - f * face, unit), 0))
    top0, bottom0, side0 = 0, nw + 2, 2 * (nw + 2)
    up_cell, down_cell = side0 + nu, side0 + nu + 1
    for n, (_, flip) in enumerate(items):
        flags[n * levels : (n + 1) * levels, :] = jnp.full((levels, LANES), flip, jnp.int32)

    lane = lax.broadcasted_iota(jnp.int32, (unit, LANES), 1)
    local_row = lax.broadcasted_iota(jnp.int32, (unit, LANES), 0)
    small_lane = lax.broadcasted_iota(jnp.int32, (8, LANES), 1)
    turn = lax.rem(
        unit - 1 - lax.broadcasted_iota(jnp.int32, (picked.shape[0], LANES), 1) + LANES, LANES
    )

    base = me * full
    up = lax.rem(i + nr - 1, nr)
    down = lax.rem(i + 1, nr)
    west = lax.rem(c + nc - 1, nc)
    east = lax.rem(c + 1, nc)

    def prepare(s, field):
        pack, stage = packs[s], stages[s]
        for l in range(levels):
            stage[0, l : l + 1, :] = field[l, 0:1, :]
            stage[1, l : l + 1, :] = field[l, rows - 1 : rows, :]
            for e, row in ((0, jnp.where(has_top, top_at, bottom_at)), (1, bottom_at)):
                line = field[l, pl.ds(row, 1), :]
                for k in range(nw):
                    part = line if k == 0 else jnp.roll(line, -k * unit, axis=1)
                    pack[base + e * nw + k, l : l + 1, :] = part
        for k in range(nu):
            both = jnp.zeros((unit, LANES), jnp.float32)
            for l in range(levels):
                block = field[l, k * unit : (k + 1) * unit, :]
                both = jnp.where(lane >= 2 * l, pltpu.roll(block, 1 + 2 * l, 1), both)
            turned = both.T
            for l in range(levels):
                last = turned[2 * l : 2 * l + 1, :]
                first = turned[2 * l + 1 : 2 * l + 2, :]
                stage[2 + k, l : l + 1, 0:unit] = first
                stage[2 + nu + k, l : l + 1, 0:unit] = last
                pack[base + side_from + k, l : l + 1, 0:unit] = jnp.where(left, first, last)

    def send(s):
        pack, stage, halo = packs[s], stages[s], halos[s]

        def near(src, dst, size, where):
            pltpu.make_async_remote_copy(
                stage.at[pl.ds(src, size)], halo.at[pl.ds(dst, size)],
                halo_send.at[s], halo_recv.at[s], device_id=where, device_id_type=MESH,
            ).start()

        def far(size):
            def step(k, carry):
                d = lax.rem(me + k, ndev)
                mine = pack.at[pl.ds(base, size)]
                pltpu.make_async_remote_copy(
                    mine, mine, pack_send.at[s], pack_recv.at[s],
                    device_id=(lax.div(d, nc), lax.rem(d, nc)), device_id_type=MESH,
                ).start()
                return carry

            lax.fori_loop(1, ndev, step, 0)

        near(0, 1, 1, (up, c))
        near(0, 5, 1, (up, west))
        near(0, 4, 1, (up, east))
        near(1, 0, 1, (down, c))
        near(1, 3, 1, (down, west))
        near(1, 2, 1, (down, east))
        near(2, 6 + nu, nu, (i, west))
        near(2 + nu, 6, nu, (i, east))

        for is_side in (True, False):
            for has_two in (True, False):
                size = (2 if has_two else 1) * nw + (nu if is_side else 0)
                pl.when(jnp.logical_and(side == is_side, both_lines == has_two))(
                    functools.partial(far, size)
                )

    doubles = sum((r * rows + offset) % face + rows > face for r in range(nr))
    everything = nc * nw * (nr + doubles) + 2 * nr * nu

    def pack_wait(s, sem, sending):
        pack = packs[s]

        def take(size):
            units = (ndev - 1) * size if sending else everything - size
            part = pack.at[pl.ds(0, units)]
            pltpu.make_async_copy(part, part, sem.at[s]).wait()

        for is_side in (True, False):
            for has_two in (True, False):
                size = (2 if has_two else 1) * nw + (nu if is_side else 0)
                pl.when(jnp.logical_and(side == is_side, both_lines == has_two))(
                    functools.partial(take, size)
                )

    def receive(s):
        halo = halos[s]
        pltpu.make_async_copy(halo, halo, halo_recv.at[s]).wait()
        pack_wait(s, pack_recv, False)

    def finish(s):
        halo = halos[s]
        pltpu.make_async_copy(halo, halo, halo_send.at[s]).wait()
        pack_wait(s, pack_send, True)

    def triple(mid, before, after):
        mid, before, after = (
            jnp.concatenate([x, jnp.zeros((8 - x.shape[0], LANES), jnp.float32)], axis=0)
            for x in (mid, before, after)
        )
        west_of = jnp.where(small_lane == 0, before, pltpu.roll(mid, 1, 1))
        east_of = jnp.where(
            small_lane == LANES - 1, pltpu.roll(after, LANES - 1, 1), pltpu.roll(mid, LANES - 1, 1)
        )
        return mid + west_of + east_of

    def partial(src, dest):
        for l in range(levels):
            for k in range(nu):
                x = src[l, k * unit : (k + 1) * unit, :]
                west_of = jnp.where(lane == 0, 0.0, pltpu.roll(x, 1, 1))
                east_of = jnp.where(lane == LANES - 1, 0.0, pltpu.roll(x, LANES - 1, 1))
                hsum[l, 8 + k * unit : 8 + (k + 1) * unit, :] = x + west_of + east_of
        for l in range(levels):
            for k in range(nu):
                r0 = k * unit
                x = src[l, r0 : r0 + unit, :]
                upper = jnp.where(
                    local_row == top_hit - r0, 0.0, hsum[l, 7 + r0 : 7 + r0 + unit, :]
                )
                lower = jnp.where(
                    local_row == bottom_hit - r0, 0.0, hsum[l, 9 + r0 : 9 + r0 + unit, :]
                )
                box = upper + hsum[l, 8 + r0 : 8 + r0 + unit, :] + lower
                dest[l, r0 : r0 + unit, :] = x + rate[r0 : r0 + unit, :] * (box - 9.0 * x)

    def gather(s):
        pack, halo = packs[s], halos[s]
        for n, (at, _) in enumerate(items):
            picked[n * levels : (n + 1) * levels, :] = pack[at]
        raw = picked[...]
        picked[...] = jnp.where(flags[...] == 1, jnp.take_along_axis(raw, turn, axis=1), raw)

        def item(n):
            return picked[n * levels : (n + 1) * levels, :]

        def whole_line(n):
            if nw == 1:
                return item(n)
            return jnp.concatenate([item(n + k)[:, 0:unit] for k in range(nw)], axis=1)

        sides = []
        blank = jnp.zeros((8 - 2 * levels, LANES), jnp.float32)
        for k in range(nu):
            own = item(side0 + k)
            w = jnp.where(left, own, halo[6 + k])
            e = jnp.where(right, own, halo[6 + nu + k])
            both = jnp.concatenate([w, e, blank], axis=0)
            sides.append(both if unit == LANES else jnp.where(small_lane < unit, both, 0.0))
        nothing = jnp.zeros((8, LANES), jnp.float32)
        beside = []
        for k in range(nu):
            r0 = k * unit
            before = sides[k - 1] if k else nothing
            after = sides[k + 1] if k < nu - 1 else nothing
            prev = jnp.where(
                small_lane == 0,
                pltpu.roll(before, (LANES + 1 - unit) % LANES, 1),
                pltpu.roll(sides[k], 1, 1),
            )
            follow = jnp.where(
                small_lane == unit - 1,
                pltpu.roll(after, unit - 1, 1),
                pltpu.roll(sides[k], LANES - 1, 1),
            )
            prev = jnp.where(small_lane == top_hit - r0, 0.0, prev)
            follow = jnp.where(small_lane == bottom_hit - r0, 0.0, follow)
            sums = sides[k] + prev + follow
            beside.append(sums if unit == LANES else jnp.where(small_lane < unit, sums, 0.0))

        ghost_top = triple(whole_line(top0), item(top0 + nw), item(top0 + nw + 1))
        ghost_bottom = triple(whole_line(bottom0), item(bottom0 + nw), item(bottom0 + nw + 1))

        def end_of(x):
            return jnp.concatenate([x[:, LANES - 1 :], x[:, : LANES - 1]], axis=1)

        above = triple(
            halo[0],
            jnp.where(left, item(up_cell), end_of(halo[2])),
            jnp.where(right, item(up_cell), halo[3]),
        )
        below = triple(
            halo[1],
            jnp.where(left, item(down_cell), end_of(halo[4])),
            jnp.where(right, item(down_cell), halo[5]),
        )
        return beside, (
            (0, top_hit != 0, above),
            (rows - 1, bottom_hit != rows - 1, below),
            (top_at, has_top, ghost_top),
            (bottom_at, has_bottom, ghost_bottom),
        )

    def complete(dest, found):
        beside, lines = found
        for k in range(nu):
            r0 = k * unit
            turned = beside[k].T[0:unit]
            scale = rate[r0 : r0 + unit, :]
            for l in range(levels):
                extra = jnp.where(
                    lane == 0,
                    turned[:, l : l + 1],
                    jnp.where(lane == LANES - 1, turned[:, levels + l : levels + l + 1], 0.0),
                )
                dest[l, r0 : r0 + unit, :] += scale * extra
        for row, used, h in lines:
            scale = rate[pl.ds(row, 1), :]
            for l in range(levels):
                more = jnp.where(used, scale * h[l : l + 1], 0.0)
                dest[l, pl.ds(row, 1), :] = dest[l, pl.ds(row, 1), :] + more

    def edge_columns(blocks_of):
        made = []
        for k in range(nu):
            both = jnp.zeros((unit, LANES), jnp.float32)
            for l in range(levels):
                block = blocks_of(l, k)
                first = block if l == 0 else pltpu.roll(block, l, 1)
                both = jnp.where(lane == l, first, both)
                both = jnp.where(lane == levels + l, pltpu.roll(block, levels + l + 1, 1), both)
            turned = both.T[0:8]
            if unit < LANES:
                blank = jnp.zeros((8, LANES - unit), jnp.float32)
                turned = jnp.concatenate([turned, blank], axis=1)
            made.append(turned)
        return made

    def prepare_next(s, dest, found, columns):
        beside, lines = found
        pack, stage = packs[s], stages[s]
        rank = lax.broadcasted_iota(jnp.int32, (8, LANES), 0)
        ends = []
        for row, used, h in lines:
            twice = h + pltpu.roll(h, levels, 0)
            at_end = small_lane == jnp.where(rank < levels, 0, LANES - 1)
            ends.append(jnp.sum(jnp.where(at_end, twice, 0.0), axis=1, keepdims=True))
        for n, (row, _, _) in enumerate(lines):
            row = jnp.where(has_top, row, bottom_at) if n == 2 else row
            near_cells = jnp.zeros((8, LANES), jnp.float32)
            for k in range(nu):
                near_cells = near_cells + jnp.where(small_lane == row - k * unit, beside[k], 0.0)
            cells = jnp.sum(near_cells, axis=1, keepdims=True) + jnp.zeros((8, LANES), jnp.float32)
            more = jnp.where(small_lane == 0, cells, 0.0) + jnp.where(
                small_lane == LANES - 1, pltpu.roll(cells, 8 - levels, 0), 0.0
            )
            for other_row, used, h in lines:
                more = more + jnp.where(jnp.logical_and(used, other_row == row), h, 0.0)
            scale = rate[pl.ds(row, 1), :]
            for l in range(levels):
                line = dest[l, pl.ds(row, 1), :] + scale * more[l : l + 1]
                if n < 2:
                    stage[n, l : l + 1, :] = line
                else:
                    for k in range(nw):
                        part = line if k == 0 else jnp.roll(line, -k * unit, axis=1)
                        pack[base + (n - 2) * nw + k, l : l + 1, :] = part
        for k in range(nu):
            total_add = beside[k]
            for (row, used, _), end in zip(lines, ends):
                at = jnp.where(used, row - k * unit, -1)
                hit = small_lane == at
                if unit < LANES:
                    hit = jnp.logical_and(hit, small_lane < unit)
                total_add = total_add + jnp.where(hit, end, 0.0)
            fresh = columns[k] + rate_columns[k] * total_add
            first, last = fresh[0:levels], fresh[levels : 2 * levels]
            stage[2 + k] = first
            stage[2 + nu + k] = last
            pack[base + side_from + k] = jnp.where(left, first, last)

    loads[0].wait()
    prepare(0, field)
    loads[1].wait()
    loads[2].wait()
    rate[...] = rate[...] * area[...] * 0.125
    pl.semaphore_wait(barrier, ndev - 1)
    for l in range(levels):
        hsum[l, 7:8, :] = jnp.zeros((1, LANES), jnp.float32)
        hsum[l, 8 + rows : 9 + rows, :] = jnp.zeros((1, LANES), jnp.float32)
    src, found = field, None
    for s in range(SWEEPS):
        final = s == SWEEPS - 1
        dest = out if final else (other if src is field else field)
        send(s)
        if s == 0:
            rate_columns = edge_columns(lambda l, k: rate[k * unit : (k + 1) * unit, :])
        else:
            complete(src, found)
        partial(src, dest)
        if not final:
            columns = edge_columns(lambda l, k: dest[l, k * unit : (k + 1) * unit, :])
        receive(s)
        found = gather(s)
        if final:
            complete(dest, found)
        else:
            prepare_next(s + 1, dest, found, columns)
        src = dest
    for s in range(SWEEPS):
        finish(s)


def on_device(noise, kappa, metric, edge_src, edge_rev, corner_src):
    levels, rows, width = noise.shape
    nr, nc = lax.axis_size("row"), lax.axis_size("col")
    unit = math.gcd(math.gcd(rows, width * nc // 2), width)
    nu, nw = rows // unit, width // unit
    count = 2 * (nw + 2) + nu + 2
    picked_rows = -(-count * levels // 8) * 8
    full = 2 * nw + nu
    scratch = [
        pltpu.VMEM((levels, rows, width), jnp.float32),
        pltpu.VMEM((levels, rows, width), jnp.float32),
        pltpu.VMEM((rows, width), jnp.float32),
        pltpu.VMEM((rows, width), jnp.float32),
        pltpu.VMEM((levels, rows + 16, width), jnp.float32),
        pltpu.VMEM((picked_rows, LANES), jnp.float32),
        pltpu.VMEM((picked_rows, LANES), jnp.int32),
    ]
    scratch += [pltpu.VMEM((nr * nc * full, levels, LANES), jnp.float32)] * SWEEPS
    scratch += [pltpu.VMEM((2 + 2 * nu, levels, LANES), jnp.float32)] * SWEEPS
    scratch += [pltpu.VMEM((6 + 2 * nu, levels, LANES), jnp.float32)] * SWEEPS
    scratch += [pltpu.SemaphoreType.DMA((6,))]
    scratch += [pltpu.SemaphoreType.DMA((SWEEPS,))] * 4
    scratch += [pltpu.SMEM(edge_src.shape, jnp.int32)] * 3
    in_hbm = pl.BlockSpec(memory_space=pltpu.HBM)
    return pl.pallas_call(
        functools.partial(kernel, (levels, rows, width, nr, nc)),
        out_shape=jax.ShapeDtypeStruct(noise.shape, jnp.float32),
        in_specs=[in_hbm] * 6,
        out_specs=pl.BlockSpec(memory_space=pltpu.VMEM),
        scratch_shapes=scratch,
        compiler_params=pltpu.CompilerParams(
            collective_id=0, has_side_effects=True, vmem_limit_bytes=48 * 1024 * 1024
        ),
    )(noise, kappa, metric, edge_src, edge_rev, corner_src)


def solution(mesh):
    in_specs = (P(None, "row", "col"), P("row", "col"), P("row", "col"), P(), P(), P())
    out_specs = P(None, "row", "col")
    return jax.shard_map(
        on_device, mesh=mesh, in_specs=in_specs, out_specs=out_specs, check_vma=False
    )
```
